256 devices in a mesh: grp: 16 (over x_hi, y, core), sub: 16 (over z, x_lo).
Axes of the slice: x: 4 (x_hi: 2, x_lo: 2; x = x_hi * 2 + x_lo), y: 4, z: 8, core: 2. Of those that a mesh axis runs over, the one named last changes fastest.
Arguments:
- basis: bfloat16 [16, 16, 270, 1152], P('grp', 'sub'), may hold values from -6 to 6
- stiffness: bfloat16 [16, 16, 1152, 1152], P('grp', 'sub'), may hold values from -0.1875 to 0.1875
- inverse: bfloat16 [16, 16, 1152, 1152], P('grp', 'sub'), may hold values from -0.1875 to 0.1875
- coupling: bfloat16 [16, 16, 4, 768, 1152], P('grp', 'sub'), may hold values from -0.109375 to 0.109375
- panel_index: int32 [16, 16, 4, 6], P('grp', 'sub'), may hold values from 0 to 8, as said below
- panel_count: int32 [16, 16, 4], P('grp', 'sub'), may hold values from 1 to 6, as said below
- owner_map: int32 [16, 16, 270], P('grp', 'sub'), may hold values from 0 to 2047, as said below
Outputs:
- coarse_matrix: float32 [2048, 2048], P(('grp', 'sub'))
The draws below stay inside these ranges and needn't reach their ends.
Inputs may be any that keep to these rules, and one draw needn't show every extreme that they name: `panel_index`: in every draw some slot names panel 9 - 1 and some names panel 0. `panel_count`: in every draw some direction has 6 live slots and some has one. Subdomain (g, s) owns the rows b * 8 to b * 8 + 7 of coarse_matrix with b = g * 16 + s; entries of owner_map may name any column, repeats allowed; column 0 and column 2048 - 1 are named in every draw.
All inputs are finite; a program needn't handle non-finite values.
Results may differ from the reference program's by a relative error of at most 0.0056.
Values may be sent and summed in bfloat16 or wider, within the bound.
A program may use at most 128 MiB of HBM per device.

```python
import jax
import jax.numpy as jnp
from jax import lax

K = 270
PANEL = 128
NB = 9
CMAX = 6
OWN = 8
N_GRP = 16
N_SUB = 16


def draw_panel_index(key, part):
    drawn = jax.random.randint(key, (N_GRP, N_SUB, 4, CMAX), 0, NB)
    return drawn.at[0, 0, 0, 0].set(NB - 1).at[0, 0, 1, 0].set(0)


def draw_panel_count(key, part):
    drawn = jax.random.randint(jax.random.fold_in(key, 7), (N_GRP, N_SUB, 4), 1, CMAX + 1)
    return drawn.at[0, 0, 0].set(CMAX).at[0, 0, 1].set(1)


def draw_owner_map(key, part):
    owners = jax.random.randint(jax.random.fold_in(key, 11), (N_GRP, N_SUB, K), 0, OWN * N_GRP * N_SUB)
    owners = owners.at[0, 0, 0].set(0).at[N_GRP - 1, N_SUB - 1, 0].set(OWN * N_GRP * N_SUB - 1)
    return owners.astype(jnp.int32)


def levels(key, extent, cuts, smallest, high):
    def one(dim, blocks):
        heights = jax.random.uniform(jax.random.fold_in(jax.random.fold_in(key, 6), dim), (blocks,), jnp.float32, smallest / len(cuts), high / len(cuts))
        return jnp.repeat(jnp.exp(heights), extent[dim] // blocks).reshape((-1,) + (1,) * (len(extent) - dim - 1))

    gain = one(*cuts[0])
    for cut in cuts[1:]:
        gain = gain * one(*cut)
    return gain


def scatter_about(own_key, extent, width, limit, shards=(), kind=jnp.bfloat16):
    values = width * jax.random.normal(own_key, extent, jnp.float32)
    if shards:
        values = values * levels(own_key, extent, shards, -0.22, 0.18)
    return jnp.clip(values, -limit, limit).astype(kind)


def setup_inputs(seed: int = 0) -> dict:
    arg_keys = jax.random.split(jax.random.key(seed), 8)
    basis = scatter_about(arg_keys[0], (N_GRP, N_SUB, K, NB * PANEL), 1.0, 6.0, ((0, 16), (1, 16)))
    stiffness = scatter_about(arg_keys[1], (N_GRP, N_SUB, NB * PANEL, NB * PANEL), (NB * PANEL) ** -0.5, 0.1875, ((0, 16), (1, 16)))
    inverse = scatter_about(arg_keys[2], (N_GRP, N_SUB, NB * PANEL, NB * PANEL), (NB * PANEL) ** -0.5, 0.1875, ((0, 16), (1, 16)))
    coupling = scatter_about(arg_keys[3], (N_GRP, N_SUB, 4, CMAX * PANEL, NB * PANEL), (4 * CMAX * PANEL) ** -0.5, 0.109375, ((0, 16), (1, 16)))
    panel_index = draw_panel_index(jax.random.fold_in(arg_keys[7], 71), 0)
    panel_count = draw_panel_count(jax.random.fold_in(arg_keys[7], 71), 0)
    owner_map = draw_owner_map(jax.random.fold_in(arg_keys[7], 71), 0)
    return dict(basis=basis, stiffness=stiffness, inverse=inverse, coupling=coupling, panel_index=panel_index, panel_count=panel_count, owner_map=owner_map)


def pick_panels(values, panel_ids, live_count):
    panels = values.reshape(values.shape[0], NB, PANEL)
    chosen = jnp.take(panels, panel_ids.astype(jnp.int32), axis=1)
    alive_mask = (jnp.arange(CMAX) < live_count).astype(values.dtype)
    return chosen * alive_mask[None, :, None]


def extend(basis, neighbours, stiffness, inverse, coupling, panel_index, panel_count):
    picked = [pick_panels(neighbours[direction], panel_index[direction], panel_count[direction]) for direction in range(4)]
    rows_margin = jnp.stack(picked, axis=1).reshape(K, 4 * CMAX * PANEL)
    margin = jnp.dot(rows_margin, coupling.reshape(4 * CMAX * PANEL, NB * PANEL), preferred_element_type=jnp.float32).astype(jnp.bfloat16)
    extension = (jnp.dot(basis, inverse, preferred_element_type=jnp.float32) + jnp.dot(margin, inverse, preferred_element_type=jnp.float32)).astype(jnp.bfloat16)
    projected = jnp.dot(extension, stiffness, preferred_element_type=jnp.float32).astype(jnp.bfloat16)
    scale_factor = float(NB * PANEL * K) ** -0.5
    return jnp.dot(projected, extension.T, preferred_element_type=jnp.float32) * scale_factor


def reference(basis, stiffness, inverse, coupling, panel_index, panel_count, owner_map):
    padded = jnp.pad(basis, ((1, 1), (1, 1), (0, 0), (0, 0)))
    neighbours = jnp.stack([padded[:-2, 1:-1], padded[2:, 1:-1], padded[1:-1, :-2], padded[1:-1, 2:]], axis=2)
    devices_all = N_GRP * N_SUB
    device_items = (
        basis.reshape(devices_all, K, NB * PANEL),
        neighbours.reshape(devices_all, 4, K, NB * PANEL),
        stiffness.reshape(devices_all, NB * PANEL, NB * PANEL),
        inverse.reshape(devices_all, NB * PANEL, NB * PANEL),
        coupling.reshape(devices_all, 4, CMAX * PANEL, NB * PANEL),
        panel_index.reshape(devices_all, 4, CMAX),
        panel_count.reshape(devices_all, 4),
        owner_map.reshape(devices_all, K),
    )

    def accumulate(running, items):
        coarse = extend(items[0], items[1], items[2], items[3], items[4], items[5], items[6])
        owners = items[7].astype(jnp.int32)
        return running.at[owners[:, None], owners[None, :]].add(coarse), None

    running = jnp.zeros((OWN * N_GRP * N_SUB, OWN * N_GRP * N_SUB), jnp.float32)
    running, unused = lax.scan(accumulate, running, device_items)
    return running
```

```python
import functools

import jax
import jax.numpy as jnp
from jax import lax
from jax.experimental import pallas as pl
from jax.experimental.pallas import tpu as pltpu
from jax.sharding import PartitionSpec as P

K = 270
PANEL = 128
NB = 9
CMAX = 6
OWN = 8
KM = 256
KR = 16
LW = 128
WIDE = 384
DEEP = 256
XL = 2
CO = 2
MESH = pl.DeviceIdType.MESH
BF16 = jnp.bfloat16
F32 = jnp.float32


def sizes(mesh_shape):
    grp, sub = mesh_shape["grp"], mesh_shape["sub"]
    xh = 2 if grp >= 16 else 1
    return xh, grp // (xh * CO), sub // XL


def kernel(
    dims, basis, reqs, own, inv_h, stiff_h, coup_h, out,
    basisp, psend, rows, rreq, acc, base, coup, inv, stiff, total, ext, proj, ct, rtp, rt, rtr,
    orecv, xsend, xrecv, acc2, keep, sibs, sibr, zsend, zrecv,
    lsem, rqs, rqr, ps, pr, os_, or_, xs, xr, ss, sr, zs, zr,
):
    XH, Y, Z = dims
    Q = XH * Y * XL
    G, S = XH * Y * CO, Z * XL
    nco = OWN * G * S
    m1 = CO * Z * OWN
    kp = KM + KR
    width = NB * PANEL
    g, s = lax.axis_index("grp"), lax.axis_index("sub")
    xh, y, co = g // (Y * CO), (g // CO) % Y, g % CO
    z, xl = s // XL, s % XL
    has = [g > 0, g < G - 1, s > 0, s < S - 1]
    face = [(g - 1, s), (g + 1, s), (g, s - 1), (g, s + 1)]
    plane = []
    for k in range(Q):
        a, b, c = k // (Y * XL), (k // XL) % Y, k % XL
        plane.append((((xh + a) % XH * Y + (y + b) % Y) * CO + co, z * XL + (xl + c) % XL))
    sibling = (g + 1 - 2 * co, s)
    column = [(g, (z + k) % Z * XL + xl) for k in range(Z)]

    loads = [pltpu.make_async_copy(coup_h.at[d], coup.at[d], lsem.at[d]) for d in range(4)]
    loads.append(pltpu.make_async_copy(inv_h, inv, lsem.at[4]))
    loads.append(pltpu.make_async_copy(stiff_h, stiff, lsem.at[5]))

    barrier = pltpu.get_barrier_semaphore()
    for d in range(4):
        @pl.when(has[d])
        def _(d=d):
            pl.semaphore_signal(barrier, inc=1, device_id=face[d], device_id_type=MESH)
    for peer in plane[1:] + [sibling] + column[1:]:
        pl.semaphore_signal(barrier, inc=1, device_id=peer, device_id_type=MESH)
    for load in loads:
        load.start()

    basisp[KM:kp, :] = jnp.zeros((KR, width), BF16)
    basisp[0:K, :] = basis[...]
    for d in range(4):
        @pl.when(jnp.logical_not(has[d]))
        def _(d=d):
            for p in range(CMAX // 2):
                rows[d * (CMAX // 2) + p] = jnp.zeros((kp, 2 * PANEL), BF16)
    orecv[0] = own[0]

    faces = sum(h.astype(jnp.int32) for h in has)
    pl.semaphore_wait(barrier, faces + (Q - 1) + 1 + (Z - 1))

    def request(d):
        return pltpu.make_async_remote_copy(
            src_ref=reqs.at[d], dst_ref=rreq.at[d ^ 1], send_sem=rqs.at[d], recv_sem=rqr.at[d ^ 1],
            device_id=face[d], device_id_type=MESH)

    def request_in(d):
        return pltpu.make_async_remote_copy(
            src_ref=reqs.at[d], dst_ref=rreq.at[d], send_sem=rqs.at[d], recv_sem=rqr.at[d],
            device_id=face[d], device_id_type=MESH)

    def panels(d, p, into):
        n = CMAX // 2
        return pltpu.make_async_remote_copy(
            src_ref=psend.at[d * n + p], dst_ref=rows.at[into * n + p], send_sem=ps.at[d * n + p],
            recv_sem=pr.at[into * n + p], device_id=face[d], device_id_type=MESH)

    def owners(k):
        return pltpu.make_async_remote_copy(
            src_ref=own.at[0], dst_ref=orecv.at[k], send_sem=os_.at[k], recv_sem=or_.at[k],
            device_id=plane[k], device_id_type=MESH)

    def spread(k):
        return pltpu.make_async_remote_copy(
            src_ref=xsend.at[k], dst_ref=xrecv.at[k], send_sem=xs.at[k], recv_sem=xr.at[k],
            device_id=plane[k], device_id_type=MESH)

    def beside():
        return pltpu.make_async_remote_copy(
            src_ref=sibs, dst_ref=sibr, send_sem=ss.at[0], recv_sem=sr.at[0],
            device_id=sibling, device_id_type=MESH)

    def along(k):
        return pltpu.make_async_remote_copy(
            src_ref=zsend.at[k], dst_ref=zrecv.at[k], send_sem=zs.at[k], recv_sem=zr.at[k],
            device_id=column[k], device_id_type=MESH)

    order = (2, 3, 0, 1)
    for d in order:
        @pl.when(has[d])
        def _(d=d):
            request(d).start()
    for k in range(1, Q):
        owners(k).start()

    def own_rows(n, carry):
        at = pl.multiple_of(n * DEEP, DEEP)
        here = lax.broadcasted_iota(jnp.int32, (DEEP, KM + LW), 0) + at
        rtp[pl.ds(at, DEEP), :] = (own[1, 0:1, :] == here).astype(F32).astype(BF16)
        return carry

    acc[...] = jnp.zeros_like(acc)

    for p in range(CMAX // 2):
        for d in order:
            @pl.when(has[d])
            def _(d=d, p=p):
                if p == 0:
                    request_in(d).wait_recv()
                for h in range(2):
                    c = 2 * p + h
                    picked = None
                    for n in range(NB):
                        mark = (rreq[d, c : c + 1, :] == n).astype(F32).astype(BF16)
                        term = basisp[:, n * PANEL : (n + 1) * PANEL] * mark
                        picked = term if picked is None else picked + term
                    psend[d * (CMAX // 2) + p, :, h * PANEL : (h + 1) * PANEL] = picked
                panels(d, p, d ^ 1).start()

    lax.fori_loop(0, nco // DEEP, own_rows, 0)
    proj[...] = jnp.zeros_like(proj)

    for k in range(1, Q):
        owners(k).wait_recv()
    packed = []
    for first in range(0, Q, LW // KR):
        line = None
        for k in range(first, min(Q, first + LW // KR)):
            piece = orecv[k, :, KM : KM + LW]
            shift = (k - first) * KR
            piece = pltpu.roll(piece, shift, 1) if shift else piece
            line = piece if line is None else line + piece
        packed.append(line[0:1, :])

    def tables(n, carry):
        at = pl.multiple_of(n * DEEP, DEEP)
        here = lax.broadcasted_iota(jnp.int32, (DEEP, KM), 0) + at
        for k in range(Q):
            rt[pl.ds(at, DEEP), k * KM : (k + 1) * KM] = (
                (orecv[k, 0:1, 0:KM] == here).astype(F32).astype(BF16))
        narrow = lax.broadcasted_iota(jnp.int32, (DEEP, LW), 0) + at
        for i, line in enumerate(packed):
            rtr[pl.ds(at, DEEP), i * LW : (i + 1) * LW] = (line == narrow).astype(F32).astype(BF16)
        return carry

    lax.fori_loop(0, nco // DEEP, tables, 0)

    loads[4].wait()

    def inner(n, carry):
        at = pl.ds(pl.multiple_of(n * WIDE, WIDE), WIDE)
        base[:, at] = jnp.dot(basisp[...], inv[:, at], preferred_element_type=F32)
        return carry

    lax.fori_loop(0, width // WIDE, inner, 0)
    for d in range(4):
        loads[d].wait()
    for p in range(CMAX // 2):
        for d in (0, 1, 2, 3):
            i = d * (CMAX // 2) + p

            @pl.when(has[d])
            def _(d=d, p=p):
                panels(d, p, d).wait_recv()

            def margin(n, carry, d=d, p=p, i=i):
                at = pl.ds(pl.multiple_of(n * WIDE, WIDE), WIDE)
                acc[:, at] += jnp.dot(
                    rows[i], coup[d, 2 * PANEL * p : 2 * PANEL * (p + 1), at],
                    preferred_element_type=F32)
                return carry

            lax.fori_loop(0, width // WIDE, margin, 0)

    loads[5].wait()
    total[...] = acc[...].astype(BF16)

    def extend(n, carry):
        at = pl.ds(pl.multiple_of(n * WIDE, WIDE), WIDE)
        outer = jnp.dot(total[...], inv[:, at], preferred_element_type=F32)
        ext[:, at] = (base[:, at] + outer).astype(BF16)
        return carry

    lax.fori_loop(0, width // WIDE, extend, 0)

    def project(n, carry):
        at = pl.ds(pl.multiple_of(n * WIDE, WIDE), WIDE)
        proj[0:kp, at] = jnp.dot(ext[...], stiff[:, at], preferred_element_type=F32).astype(BF16)
        return carry

    lax.fori_loop(0, width // WIDE, project, 0)
    scale = float(width * K) ** (-0.5)
    ct[...] = (
        lax.dot_general(ext[...], proj[...], (((1,), (1,)), ((), ())), preferred_element_type=F32)
        * scale
    ).astype(BF16)

    for k in list(range(Q - 1, 0, -1)) + [0]:
        xsend[k] = lax.dot_general(
            ct[...], rtp[k * m1 : (k + 1) * m1, :], (((1,), (1,)), ((), ())),
            preferred_element_type=F32).astype(BF16)
        if k:
            spread(k).start()
    xrecv[0] = xsend[0]

    def add(table, lanes, block, first):
        def step(n, carry):
            at = pl.ds(pl.multiple_of(n * DEEP, DEEP), DEEP)
            term = jnp.dot(table[at, lanes], block, preferred_element_type=F32)
            acc2[at, :] = term if first else acc2[at, :] + term
            return carry

        lax.fori_loop(0, nco // DEEP, step, 0)

    for k in [0] + list(range(Q - 1, 0, -1)):
        if k:
            spread(k).wait_recv()
        add(rt, slice(k * KM, (k + 1) * KM), xrecv[k, 0:KM, :], k == 0)
    rest = jnp.concatenate([xrecv[k, KM:kp, :] for k in range(Q)], axis=0)
    if rtr.shape[1] > Q * KR:
        rest = jnp.concatenate([rest, jnp.zeros((rtr.shape[1] - Q * KR, m1), BF16)], axis=0)
    add(rtr, slice(0, rtr.shape[1]), rest, False)

    half = m1 // 2
    for n in range(nco // DEEP):
        at = slice(n * DEEP, (n + 1) * DEEP)
        turned = jnp.transpose(acc2[at, :])
        keep[:, at] = turned[0:half, :]
        sibs[:, at] = turned[half:, :]
    beside().start()
    beside().wait_recv()
    keep[...] += sibr[...]
    mid = nco // 2
    for k in range(1, Z):
        piece = keep[k * OWN : (k + 1) * OWN, :]
        zsend[k] = jnp.concatenate([piece[:, :mid], piece[:, mid:]], axis=0).astype(BF16)
        along(k).start()
    result = jnp.concatenate([keep[0:OWN, :mid], keep[0:OWN, mid:]], axis=0)
    for k in range(1, Z):
        along(k).wait_recv()
        result = result + zrecv[k].astype(F32)
    out[:, :mid] = result[0:OWN, :]
    out[:, mid:] = result[OWN:, :]

    for d in range(4):
        @pl.when(has[d])
        def _(d=d):
            request(d).wait_send()
            for p in range(CMAX // 2):
                panels(d, p, d ^ 1).wait_send()
    for k in range(1, Q):
        owners(k).wait_send()
        spread(k).wait_send()
    beside().wait_send()
    for k in range(1, Z):
        along(k).wait_send()


def shards(dims, basis, stiffness, inverse, coupling, panel_index, panel_count, owner_map):
    XH, Y, Z = dims
    Q = XH * Y * XL
    nco = OWN * XH * Y * CO * Z * XL
    m1 = CO * Z * OWN
    kp = KM + KR
    width = NB * PANEL
    g, s = lax.axis_index("grp"), lax.axis_index("sub")
    slots = jnp.arange(8, dtype=jnp.int32)
    wanted = jnp.pad(panel_index[0, 0], ((0, 0), (0, 8 - CMAX)))
    wanted = jnp.where(slots[None, :] < panel_count[0, 0][:, None], wanted, -1)
    reqs = jnp.broadcast_to(wanted[:, :, None], (4, 8, PANEL))

    m = owner_map[0, 0]
    mg, ms = m // (OWN * XL * Z), (m // OWN) % (XL * Z)
    a = (mg // (Y * CO) - g // (Y * CO)) % XH
    b = ((mg // CO) % Y - (g // CO) % Y) % Y
    c = (ms % XL - s % XL) % XL
    side = (mg % CO - g % CO) % CO
    up = (ms // XL - s // XL) % Z
    place = ((((a * Y + b) * XL + c) * CO + side) * Z + up) * OWN + m % OWN
    lines = jnp.stack([m, place])
    lines = jnp.pad(lines, ((0, 0), (0, kp - K)), constant_values=-1)
    lines = jnp.pad(lines, ((0, 0), (0, KM + LW - kp)))
    own = jnp.broadcast_to(lines[:, None, :], (2, 8, KM + LW))

    n = CMAX // 2
    packed = -(-Q * KR // LW) * LW
    vmem = pl.BlockSpec(memory_space=pltpu.VMEM)
    hbm = pl.BlockSpec(memory_space=pl.ANY)
    dma = pltpu.SemaphoreType.DMA
    return pl.pallas_call(
        functools.partial(kernel, dims),
        out_shape=jax.ShapeDtypeStruct((OWN, nco), F32),
        in_specs=[vmem, vmem, vmem, hbm, hbm, hbm],
        out_specs=vmem,
        scratch_shapes=[
            pltpu.VMEM((kp, width), BF16),
            pltpu.VMEM((4 * n, kp, 2 * PANEL), BF16),
            pltpu.VMEM((4 * n, kp, 2 * PANEL), BF16),
            pltpu.VMEM((4, 8, PANEL), jnp.int32),
            pltpu.VMEM((kp, width), F32),
            pltpu.VMEM((kp, width), F32),
            pltpu.VMEM((4, CMAX * PANEL, width), BF16),
            pltpu.VMEM((width, width), BF16),
            pltpu.VMEM((width, width), BF16),
            pltpu.VMEM((kp, width), BF16),
            pltpu.VMEM((kp, width), BF16),
            pltpu.VMEM((KM + LW, width), BF16),
            pltpu.VMEM((kp, KM + LW), BF16),
            pltpu.VMEM((nco, KM + LW), BF16),
            pltpu.VMEM((nco, Q * KM), BF16),
            pltpu.VMEM((nco, packed), BF16),
            pltpu.VMEM((Q, 8, KM + LW), jnp.int32),
            pltpu.VMEM((Q, kp, m1), BF16),
            pltpu.VMEM((Q, kp, m1), BF16),
            pltpu.VMEM((nco, m1), F32),
            pltpu.VMEM((m1 // 2, nco), F32),
            pltpu.VMEM((m1 // 2, nco), F32),
            pltpu.VMEM((m1 // 2, nco), F32),
            pltpu.VMEM((Z, 2 * OWN, nco // 2), BF16),
            pltpu.VMEM((Z, 2 * OWN, nco // 2), BF16),
            dma((6,)), dma((4,)), dma((4,)), dma((4 * n,)), dma((4 * n,)),
            dma((Q,)), dma((Q,)), dma((Q,)), dma((Q,)), dma((1,)), dma((1,)), dma((Z,)), dma((Z,)),
        ],
        compiler_params=pltpu.CompilerParams(
            collective_id=0, has_side_effects=True, vmem_limit_bytes=58 * 2**20
        ),
    )(basis[0, 0], reqs, own, inverse[0, 0], stiffness[0, 0], coupling[0, 0])


def solution(mesh):
    in_specs = (
        P("grp", "sub", None, None),
        P("grp", "sub", None, None),
        P("grp", "sub", None, None),
        P("grp", "sub", None, None, None),
        P("grp", "sub", None, None),
        P("grp", "sub", None),
        P("grp", "sub", None),
    )
    return jax.shard_map(
        functools.partial(shards, sizes(mesh.shape)),
        mesh=mesh, in_specs=in_specs, out_specs=P(("grp", "sub"), None), check_vma=False,
    )
```

```python
import functools

import jax
import jax.numpy as jnp
from jax import lax
from jax.experimental import pallas as pl
from jax.experimental.pallas import tpu as pltpu
from jax.sharding import PartitionSpec as P

K = 270
PANEL = 128
NB = 9
CMAX = 6
OWN = 8
KM = 256
KR = 16
LW = 128
WIDE = 384
DEEP = 256
XL = 2
CO = 2
MESH = pl.DeviceIdType.MESH
BF16 = jnp.bfloat16
F32 = jnp.float32


def sizes(mesh_shape):
    grp, sub = mesh_shape["grp"], mesh_shape["sub"]
    xh = 2 if grp >= 16 else 1
    return xh, grp // (xh * CO), sub // XL


def kernel(
    dims, basis, index, count, owner, inv_h, stiff_h, coup_h, out,
    basisp, reqs, own, psend, rows, rreq, acc, base, coup, inv, stiff, total, ext, proj, ct, rtp, rt, rtr,
    orecv, xsend, xrecv, acc2, keep, sibs, sibr, zsend, zrecv,
    lsem, rqs, rqr, ps, pr, os_, or_, xs, xr, ss, sr, zs, zr,
):
    XH, Y, Z = dims
    Q = XH * Y * XL
    G, S = XH * Y * CO, Z * XL
    nco = OWN * G * S
    m1 = CO * Z * OWN
    kp = KM + KR
    width = NB * PANEL
    g, s = lax.axis_index("grp"), lax.axis_index("sub")
    xh, y, co = g // (Y * CO), (g // CO) % Y, g % CO
    z, xl = s // XL, s % XL
    has = [g > 0, g < G - 1, s > 0, s < S - 1]
    face = [(g - 1, s), (g + 1, s), (g, s - 1), (g, s + 1)]
    plane = []
    for k in range(Q):
        a, b, c = k // (Y * XL), (k // XL) % Y, k % XL
        plane.append((((xh + a) % XH * Y + (y + b) % Y) * CO + co, z * XL + (xl + c) % XL))
    sibling = (g + 1 - 2 * co, s)
    column = [(g, (z + k) % Z * XL + xl) for k in range(Z)]

    loads = [pltpu.make_async_copy(coup_h.at[d], coup.at[d], lsem.at[d]) for d in range(4)]
    loads.append(pltpu.make_async_copy(inv_h, inv, lsem.at[4]))
    loads.append(pltpu.make_async_copy(stiff_h, stiff, lsem.at[5]))

    barrier = pltpu.get_barrier_semaphore()
    for d in range(4):
        @pl.when(has[d])
        def _(d=d):
            pl.semaphore_signal(barrier, inc=1, device_id=face[d], device_id_type=MESH)
    for peer in plane[1:] + [sibling] + column[1:]:
        pl.semaphore_signal(barrier, inc=1, device_id=peer, device_id_type=MESH)
    for load in loads:
        load.start()

    basisp[KM:kp, :] = jnp.zeros((KR, width), BF16)
    basisp[0:K, :] = basis[...]
    for d in range(4):
        @pl.when(jnp.logical_not(has[d]))
        def _(d=d):
            for p in range(CMAX // 2):
                rows[d * (CMAX // 2) + p] = jnp.zeros((kp, 2 * PANEL), BF16)
    for d in range(4):
        for c in range(CMAX):
            wanted = jnp.where(c < count[0, d], index[d, c], -1)
            reqs[d, c : c + 1, :] = jnp.full((1, LW), wanted, jnp.int32)
    own[0] = jnp.zeros((8, KM + LW), jnp.int32)
    own[0, 0:1, 0:K] = owner[...]
    m = jnp.broadcast_to(own[0, 0:1, :], (8, KM + LW))
    own[0] = m
    orecv[0] = m
    bits = [n.bit_length() - 1 for n in (XL, Z, CO, Y, XH)]
    ms, mg = m >> 3, m >> (3 + bits[0] + bits[1])
    there = ((mg >> (bits[2] + bits[3])) - xh) & (XH - 1)
    there = (there << bits[3]) + (((mg >> bits[2]) - y) & (Y - 1))
    there = (there << bits[0]) + ((ms - xl) & (XL - 1))
    there = (there << bits[2]) + ((mg - co) & (CO - 1))
    there = (there << bits[1]) + (((ms >> bits[0]) - z) & (Z - 1))
    own[1] = (there << 3) + (m & 7)

    faces = sum(h.astype(jnp.int32) for h in has)
    pl.semaphore_wait(barrier, faces + (Q - 1) + 1 + (Z - 1))

    def request(d):
        return pltpu.make_async_remote_copy(
            src_ref=reqs.at[d], dst_ref=rreq.at[d ^ 1], send_sem=rqs.at[d], recv_sem=rqr.at[d ^ 1],
            device_id=face[d], device_id_type=MESH)

    def request_in(d):
        return pltpu.make_async_remote_copy(
            src_ref=reqs.at[d], dst_ref=rreq.at[d], send_sem=rqs.at[d], recv_sem=rqr.at[d],
            device_id=face[d], device_id_type=MESH)

    def panels(d, p, into):
        n = CMAX // 2
        return pltpu.make_async_remote_copy(
            src_ref=psend.at[d * n + p], dst_ref=rows.at[into * n + p], send_sem=ps.at[d * n + p],
            recv_sem=pr.at[into * n + p], device_id=face[d], device_id_type=MESH)

    def owners(k):
        return pltpu.make_async_remote_copy(
            src_ref=own.at[0], dst_ref=orecv.at[k], send_sem=os_.at[k], recv_sem=or_.at[k],
            device_id=plane[k], device_id_type=MESH)

    def spread(k):
        return pltpu.make_async_remote_copy(
            src_ref=xsend.at[k], dst_ref=xrecv.at[k], send_sem=xs.at[k], recv_sem=xr.at[k],
            device_id=plane[k], device_id_type=MESH)

    def beside():
        return pltpu.make_async_remote_copy(
            src_ref=sibs, dst_ref=sibr, send_sem=ss.at[0], recv_sem=sr.at[0],
            device_id=sibling, device_id_type=MESH)

    def along(k):
        return pltpu.make_async_remote_copy(
            src_ref=zsend.at[k], dst_ref=zrecv.at[k], send_sem=zs.at[k], recv_sem=zr.at[k],
            device_id=column[k], device_id_type=MESH)

    order = (2, 3, 0, 1)
    for d in order:
        @pl.when(has[d])
        def _(d=d):
            request(d).start()
    for k in range(1, Q):
        owners(k).start()

    def own_rows(n, carry):
        at = pl.multiple_of(n * DEEP, DEEP)
        here = lax.broadcasted_iota(jnp.int32, (DEEP, KM + LW), 0) + at
        rtp[pl.ds(at, DEEP), :] = (own[1, 0:1, :] == here).astype(F32).astype(BF16)
        return carry

    acc[...] = jnp.zeros_like(acc)

    for p in range(CMAX // 2):
        for d in order:
            @pl.when(has[d])
            def _(d=d, p=p):
                if p == 0:
                    request_in(d).wait_recv()
                for h in range(2):
                    c = 2 * p + h
                    picked = None
                    for n in range(NB):
                        mark = (rreq[d, c : c + 1, 0:PANEL] == n).astype(F32).astype(BF16)
                        term = basisp[:, n * PANEL : (n + 1) * PANEL] * mark
                        picked = term if picked is None else picked + term
                    psend[d * (CMAX // 2) + p, :, h * PANEL : (h + 1) * PANEL] = picked
                panels(d, p, d ^ 1).start()

    lax.fori_loop(0, nco // DEEP, own_rows, 0)
    proj[...] = jnp.zeros_like(proj)

    for k in range(1, Q):
        owners(k).wait_recv()
    packed = []
    for first in range(0, Q, LW // KR):
        line = None
        for k in range(first, min(Q, first + LW // KR)):
            piece = orecv[k, :, KM : KM + LW]
            shift = (k - first) * KR
            piece = pltpu.roll(piece, shift, 1) if shift else piece
            line = piece if line is None else line + piece
        packed.append(line[0:1, :])

    def tables(n, carry):
        at = pl.multiple_of(n * DEEP, DEEP)
        here = lax.broadcasted_iota(jnp.int32, (DEEP, KM), 0) + at
        for k in range(Q):
            rt[pl.ds(at, DEEP), k * KM : (k + 1) * KM] = (
                (orecv[k, 0:1, 0:KM] == here).astype(F32).astype(BF16))
        narrow = lax.broadcasted_iota(jnp.int32, (DEEP, LW), 0) + at
        for i, line in enumerate(packed):
            rtr[pl.ds(at, DEEP), i * LW : (i + 1) * LW] = (line == narrow).astype(F32).astype(BF16)
        return carry

    lax.fori_loop(0, nco // DEEP, tables, 0)

    loads[4].wait()

    def inner(n, carry):
        at = pl.ds(pl.multiple_of(n * WIDE, WIDE), WIDE)
        base[:, at] = jnp.dot(basisp[...], inv[:, at], preferred_element_type=F32)
        return carry

    lax.fori_loop(0, width // WIDE, inner, 0)
    for d in range(4):
        loads[d].wait()
    for p in range(CMAX // 2):
        for d in (0, 1, 2, 3):
            i = d * (CMAX // 2) + p

            @pl.when(has[d])
            def _(d=d, p=p):
                panels(d, p, d).wait_recv()

            acc[...] += jnp.dot(
                rows[i], coup[d, 2 * PANEL * p : 2 * PANEL * (p + 1), :],
                preferred_element_type=F32)

    loads[5].wait()
    total[...] = acc[...].astype(BF16)

    outer = jnp.dot(total[...], inv[...], preferred_element_type=F32)
    ext[...] = (base[...] + outer).astype(BF16)
    proj[0:kp, :] = jnp.dot(ext[...], stiff[...], preferred_element_type=F32).astype(BF16)
    scale = float(width * K) ** (-0.5)
    ct[...] = (
        lax.dot_general(ext[...], proj[...], (((1,), (1,)), ((), ())), preferred_element_type=F32)
        * scale
    ).astype(BF16)

    for k in list(range(Q - 1, 0, -1)) + [0]:
        xsend[k] = lax.dot_general(
            ct[...], rtp[k * m1 : (k + 1) * m1, :], (((1,), (1,)), ((), ())),
            preferred_element_type=F32).astype(BF16)
        if k:
            spread(k).start()
    xrecv[0] = xsend[0]

    def spread_from(k):
        return pltpu.make_async_remote_copy(
            src_ref=xsend.at[k], dst_ref=xrecv.at[k], send_sem=xs.at[k], recv_sem=xr.at[k],
            device_id=sibling, device_id_type=MESH)

    acc2[...] = jnp.dot(rt[:, 0:KM], xrecv[0, 0:KM, :], preferred_element_type=F32)

    def add(n, carry):
        k = Q - n
        spread_from(k).wait_recv()
        lanes = pl.ds(pl.multiple_of(k * KM, KM), KM)
        acc2[...] += jnp.dot(rt[:, lanes], xrecv[k, 0:KM, :], preferred_element_type=F32)
        return carry

    lax.fori_loop(1, Q, add, 0)
    rest = jnp.concatenate([xrecv[k, KM:kp, :] for k in range(Q)], axis=0)
    if rtr.shape[1] > Q * KR:
        rest = jnp.concatenate([rest, jnp.zeros((rtr.shape[1] - Q * KR, m1), BF16)], axis=0)
    acc2[...] += jnp.dot(rtr[...], rest, preferred_element_type=F32)

    half = m1 // 2
    for n in range(nco // DEEP):
        at = slice(n * DEEP, (n + 1) * DEEP)
        turned = jnp.transpose(acc2[at, :])
        keep[:, at] = turned[0:half, :]
        sibs[:, at] = turned[half:, :]
    beside().start()
    beside().wait_recv()
    keep[...] += sibr[...]
    mid = nco // 2
    for k in range(1, Z):
        piece = keep[k * OWN : (k + 1) * OWN, :]
        zsend[k] = jnp.concatenate([piece[:, :mid], piece[:, mid:]], axis=0).astype(BF16)
        along(k).start()
    result = jnp.concatenate([keep[0:OWN, :mid], keep[0:OWN, mid:]], axis=0)
    for k in range(1, Z):
        along(k).wait_recv()
        result = result + zrecv[k].astype(F32)
    out[:, :mid] = result[0:OWN, :]
    out[:, mid:] = result[OWN:, :]

    for d in range(4):
        @pl.when(has[d])
        def _(d=d):
            request(d).wait_send()
            for p in range(CMAX // 2):
                panels(d, p, d ^ 1).wait_send()
    for k in range(1, Q):
        owners(k).wait_send()
        spread(k).wait_send()
    beside().wait_send()
    for k in range(1, Z):
        along(k).wait_send()


def shards(dims, basis, stiffness, inverse, coupling, panel_index, panel_count, owner_map):
    XH, Y, Z = dims
    Q = XH * Y * XL
    nco = OWN * XH * Y * CO * Z * XL
    m1 = CO * Z * OWN
    kp = KM + KR
    width = NB * PANEL
    n = CMAX // 2
    packed = -(-Q * KR // LW) * LW
    vmem = pl.BlockSpec(memory_space=pltpu.VMEM)
    smem = pl.BlockSpec(memory_space=pltpu.SMEM)
    hbm = pl.BlockSpec(memory_space=pl.ANY)
    dma = pltpu.SemaphoreType.DMA
    return pl.pallas_call(
        functools.partial(kernel, dims),
        out_shape=jax.ShapeDtypeStruct((OWN, nco), F32),
        in_specs=[vmem, smem, smem, vmem, hbm, hbm, hbm],
        out_specs=vmem,
        scratch_shapes=[
            pltpu.VMEM((kp, width), BF16),
            pltpu.VMEM((4, 8, LW), jnp.int32),
            pltpu.VMEM((2, 8, KM + LW), jnp.int32),
            pltpu.VMEM((4 * n, kp, 2 * PANEL), BF16),
            pltpu.VMEM((4 * n, kp, 2 * PANEL), BF16),
            pltpu.VMEM((4, 8, LW), jnp.int32),
            pltpu.VMEM((kp, width), F32),
            pltpu.VMEM((kp, width), F32),
            pltpu.VMEM((4, CMAX * PANEL, width), BF16),
            pltpu.VMEM((width, width), BF16),
            pltpu.VMEM((width, width), BF16),
            pltpu.VMEM((kp, width), BF16),
            pltpu.VMEM((kp, width), BF16),
            pltpu.VMEM((KM + LW, width), BF16),
            pltpu.VMEM((kp, KM + LW), BF16),
            pltpu.VMEM((nco, KM + LW), BF16),
            pltpu.VMEM((nco, Q * KM), BF16),
            pltpu.VMEM((nco, packed), BF16),
            pltpu.VMEM((Q, 8, KM + LW), jnp.int32),
            pltpu.VMEM((Q, kp, m1), BF16),
            pltpu.VMEM((Q, kp, m1), BF16),
            pltpu.VMEM((nco, m1), F32),
            pltpu.VMEM((m1 // 2, nco), F32),
            pltpu.VMEM((m1 // 2, nco), F32),
            pltpu.VMEM((m1 // 2, nco), F32),
            pltpu.VMEM((Z, 2 * OWN, nco // 2), BF16),
            pltpu.VMEM((Z, 2 * OWN, nco // 2), BF16),
            dma((6,)), dma((4,)), dma((4,)), dma((4 * n,)), dma((4 * n,)),
            dma((Q,)), dma((Q,)), dma((Q,)), dma((Q,)), dma((1,)), dma((1,)), dma((Z,)), dma((Z,)),
        ],
        compiler_params=pltpu.CompilerParams(
            collective_id=0, has_side_effects=True, vmem_limit_bytes=58 * 2**20
        ),
    )(basis[0, 0], panel_index[0, 0], panel_count[0], owner_map[0], inverse[0, 0], stiffness[0, 0], coupling[0, 0])


def solution(mesh):
    in_specs = (
        P("grp", "sub", None, None),
        P("grp", "sub", None, None),
        P("grp", "sub", None, None),
        P("grp", "sub", None, None, None),
        P("grp", "sub", None, None),
        P("grp", "sub", None),
        P("grp", "sub", None),
    )
    return jax.shard_map(
        functools.partial(shards, sizes(mesh.shape)),
        mesh=mesh, in_specs=in_specs, out_specs=P(("grp", "sub"), None), check_vma=False,
    )
```

```python
import functools

import jax
import jax.numpy as jnp
from jax import lax
from jax.experimental import pallas as pl
from jax.experimental.pallas import tpu as pltpu
from jax.sharding import PartitionSpec as P

K = 270
PANEL = 128
NB = 9
CMAX = 6
OWN = 8
KM = 256
KR = 16
LW = 128
WIDE = 384
DEEP = 256
XL = 2
CO = 2
MESH = pl.DeviceIdType.MESH
BF16 = jnp.bfloat16
F32 = jnp.float32


def sizes(mesh_shape):
    grp, sub = mesh_shape["grp"], mesh_shape["sub"]
    xh = 2 if grp >= 16 else 1
    return xh, grp // (xh * CO), sub // XL


def kernel(
    dims, basis, index, count, owner, inv_h, stiff_h, coup_h, out,
    basisp, reqs, own, psend, rows, rreq, acc, base, coup, inv, stiff, total, ext, proj, ct, rtp, rt, rtr,
    orecv, xsend, xrecv, acc2, keep, sibs, sibr, zsend, zrecv,
    lsem, rqs, rqr, ps, pr, os_, or_, xs, xr, ss, sr, zs, zr,
):
    XH, Y, Z = dims
    Q = XH * Y * XL
    G, S = XH * Y * CO, Z * XL
    nco = OWN * G * S
    m1 = CO * Z * OWN
    kp = KM + KR
    width = NB * PANEL
    g, s = lax.axis_index("grp"), lax.axis_index("sub")
    xh, y, co = g // (Y * CO), (g // CO) % Y, g % CO
    z, xl = s // XL, s % XL
    has = [g > 0, g < G - 1, s > 0, s < S - 1]
    face = [(g - 1, s), (g + 1, s), (g, s - 1), (g, s + 1)]
    plane = []
    for k in range(Q):
        a, b, c = k // (Y * XL), (k // XL) % Y, k % XL
        plane.append((((xh + a) % XH * Y + (y + b) % Y) * CO + co, z * XL + (xl + c) % XL))
    sibling = (g + 1 - 2 * co, s)
    column = [(g, (z + k) % Z * XL + xl) for k in range(Z)]

    loads = [pltpu.make_async_copy(coup_h.at[d], coup.at[d], lsem.at[d]) for d in range(4)]
    loads.append(pltpu.make_async_copy(inv_h, inv, lsem.at[4]))
    loads.append(pltpu.make_async_copy(stiff_h, stiff, lsem.at[5]))

    barrier = pltpu.get_barrier_semaphore()
    for d in range(4):
        @pl.when(has[d])
        def _(d=d):
            pl.semaphore_signal(barrier, inc=1, device_id=face[d], device_id_type=MESH)
    for peer in plane[1:] + [sibling] + column[1:]:
        pl.semaphore_signal(barrier, inc=1, device_id=peer, device_id_type=MESH)
    for load in loads:
        load.start()

    basisp[KM:kp, :] = jnp.zeros((KR, width), BF16)
    basisp[0:K, :] = basis[...]
    for d in range(4):
        @pl.when(jnp.logical_not(has[d]))
        def _(d=d):
            for p in range(CMAX // 2):
                rows[d * (CMAX // 2) + p] = jnp.zeros((kp, 2 * PANEL), BF16)
    for d in range(4):
        for c in range(CMAX):
            wanted = jnp.where(c < count[0, d], index[d, c], -1)
            reqs[d, c : c + 1, :] = jnp.full((1, LW), wanted, jnp.int32)
    own[0] = jnp.zeros((8, KM + LW), jnp.int32)
    own[0, 0:1, 0:K] = owner[...]
    m = jnp.broadcast_to(own[0, 0:1, :], (8, KM + LW))
    own[0] = m
    orecv[0] = m
    bits = [n.bit_length() - 1 for n in (XL, Z, CO, Y, XH)]
    ms, mg = m >> 3, m >> (3 + bits[0] + bits[1])
    there = ((mg >> (bits[2] + bits[3])) - xh) & (XH - 1)
    there = (there << bits[3]) + (((mg >> bits[2]) - y) & (Y - 1))
    there = (there << bits[0]) + ((ms - xl) & (XL - 1))
    there = (there << bits[2]) + ((mg - co) & (CO - 1))
    there = (there << bits[1]) + (((ms >> bits[0]) - z) & (Z - 1))
    own[1] = (there << 3) + (m & 7)

    faces = sum(h.astype(jnp.int32) for h in has)
    pl.semaphore_wait(barrier, faces + (Q - 1) + 1 + (Z - 1))

    def request(d):
        return pltpu.make_async_remote_copy(
            src_ref=reqs.at[d], dst_ref=rreq.at[d ^ 1], send_sem=rqs.at[d], recv_sem=rqr.at[d ^ 1],
            device_id=face[d], device_id_type=MESH)

    def request_in(d):
        return pltpu.make_async_remote_copy(
            src_ref=reqs.at[d], dst_ref=rreq.at[d], send_sem=rqs.at[d], recv_sem=rqr.at[d],
            device_id=face[d], device_id_type=MESH)

    def panels(d, p, into):
        n = CMAX // 2
        return pltpu.make_async_remote_copy(
            src_ref=psend.at[d * n + p], dst_ref=rows.at[into * n + p], send_sem=ps.at[d * n + p],
            recv_sem=pr.at[into * n + p], device_id=face[d], device_id_type=MESH)

    def owners(k):
        return pltpu.make_async_remote_copy(
            src_ref=own.at[0], dst_ref=orecv.at[k], send_sem=os_.at[k], recv_sem=or_.at[k],
            device_id=plane[k], device_id_type=MESH)

    def spread(k):
        return pltpu.make_async_remote_copy(
            src_ref=xsend.at[k], dst_ref=xrecv.at[k], send_sem=xs.at[k], recv_sem=xr.at[k],
            device_id=plane[k], device_id_type=MESH)

    def beside(h):
        return pltpu.make_async_remote_copy(
            src_ref=sibs.at[h], dst_ref=sibr.at[h], send_sem=ss.at[h], recv_sem=sr.at[h],
            device_id=sibling, device_id_type=MESH)

    def along(h, k):
        i = h * Z + k
        return pltpu.make_async_remote_copy(
            src_ref=zsend.at[i], dst_ref=zrecv.at[i], send_sem=zs.at[i], recv_sem=zr.at[i],
            device_id=column[k], device_id_type=MESH)

    order = (2, 3, 0, 1)
    for d in order:
        @pl.when(has[d])
        def _(d=d):
            request(d).start()
    for k in range(1, Q):
        owners(k).start()

    def own_rows(n, carry):
        at = pl.multiple_of(n * DEEP, DEEP)
        here = lax.broadcasted_iota(jnp.int32, (DEEP, KM + LW), 0) + at
        rtp[pl.ds(at, DEEP), :] = (own[1, 0:1, :] == here).astype(F32).astype(BF16)
        return carry

    acc[...] = jnp.zeros_like(acc)

    for p in range(CMAX // 2):
        for d in order:
            @pl.when(has[d])
            def _(d=d, p=p):
                if p == 0:
                    request_in(d).wait_recv()
                for h in range(2):
                    c = 2 * p + h
                    picked = None
                    for n in range(NB):
                        mark = (rreq[d, c : c + 1, 0:PANEL] == n).astype(F32).astype(BF16)
                        term = basisp[:, n * PANEL : (n + 1) * PANEL] * mark
                        picked = term if picked is None else picked + term
                    psend[d * (CMAX // 2) + p, :, h * PANEL : (h + 1) * PANEL] = picked
                panels(d, p, d ^ 1).start()

    lax.fori_loop(0, nco // DEEP, own_rows, 0)
    proj[...] = jnp.zeros_like(proj)

    for k in range(1, Q):
        owners(k).wait_recv()
    packed = []
    for first in range(0, Q, LW // KR):
        line = None
        for k in range(first, min(Q, first + LW // KR)):
            piece = orecv[k, :, KM : KM + LW]
            shift = (k - first) * KR
            piece = pltpu.roll(piece, shift, 1) if shift else piece
            line = piece if line is None else line + piece
        packed.append(line[0:1, :])

    def tables(n, carry):
        at = pl.multiple_of(n * DEEP, DEEP)
        here = lax.broadcasted_iota(jnp.int32, (DEEP, KM), 0) + at
        for k in range(Q):
            rt[pl.ds(at, DEEP), k * KM : (k + 1) * KM] = (
                (orecv[k, 0:1, 0:KM] == here).astype(F32).astype(BF16))
        narrow = lax.broadcasted_iota(jnp.int32, (DEEP, LW), 0) + at
        for i, line in enumerate(packed):
            rtr[pl.ds(at, DEEP), i * LW : (i + 1) * LW] = (line == narrow).astype(F32).astype(BF16)
        return carry

    lax.fori_loop(0, nco // DEEP, tables, 0)

    loads[4].wait()

    def inner(n, carry):
        at = pl.ds(pl.multiple_of(n * WIDE, WIDE), WIDE)
        base[:, at] = jnp.dot(basisp[...], inv[:, at], preferred_element_type=F32)
        return carry

    lax.fori_loop(0, width // WIDE, inner, 0)
    for d in range(4):
        loads[d].wait()
    for p in range(CMAX // 2):
        for d in (0, 1, 2, 3):
            i = d * (CMAX // 2) + p

            @pl.when(has[d])
            def _(d=d, p=p):
                panels(d, p, d).wait_recv()

            acc[...] += jnp.dot(
                rows[i], coup[d, 2 * PANEL * p : 2 * PANEL * (p + 1), :],
                preferred_element_type=F32)

    loads[5].wait()
    total[...] = acc[...].astype(BF16)

    outer = jnp.dot(total[...], inv[...], preferred_element_type=F32)
    ext[...] = (base[...] + outer).astype(BF16)
    proj[0:kp, :] = jnp.dot(ext[...], stiff[...], preferred_element_type=F32).astype(BF16)
    scale = float(width * K) ** (-0.5)
    ct[...] = (
        lax.dot_general(ext[...], proj[...], (((1,), (1,)), ((), ())), preferred_element_type=F32)
        * scale
    ).astype(BF16)

    for k in range(Q - 2, -1, -2):
        pair = lax.dot_general(
            ct[...], rtp[k * m1 : (k + 2) * m1, :], (((1,), (1,)), ((), ())),
            preferred_element_type=F32).astype(BF16)
        xsend[k + 1] = pair[:, m1:]
        spread(k + 1).start()
        xsend[k] = pair[:, :m1]
        if k:
            spread(k).start()
    xrecv[0] = xsend[0]

    def spread_from(k):
        return pltpu.make_async_remote_copy(
            src_ref=xsend.at[k], dst_ref=xrecv.at[k], send_sem=xs.at[k], recv_sem=xr.at[k],
            device_id=sibling, device_id_type=MESH)

    acc2[...] = jnp.dot(rt[:, 0:KM], xrecv[0, 0:KM, :], preferred_element_type=F32)

    def add(n, carry):
        k = Q - n
        spread_from(k).wait_recv()
        lanes = pl.ds(pl.multiple_of(k * KM, KM), KM)
        acc2[...] += jnp.dot(rt[:, lanes], xrecv[k, 0:KM, :], preferred_element_type=F32)
        return carry

    lax.fori_loop(1, Q, add, 0)
    rest = jnp.concatenate([xrecv[k, KM:kp, :] for k in range(Q)], axis=0)
    if rtr.shape[1] > Q * KR:
        rest = jnp.concatenate([rest, jnp.zeros((rtr.shape[1] - Q * KR, m1), BF16)], axis=0)
    acc2[...] += jnp.dot(rtr[...], rest, preferred_element_type=F32)

    half, mid, quarter = m1 // 2, nco // 2, nco // 4
    far = sorted(range(1, Z), key=lambda k: abs(2 * k - Z))
    for h in range(2):
        for n in range(0, mid, DEEP):
            at = h * mid + n
            turned = jnp.transpose(acc2[at : at + DEEP, :])
            keep[:, at : at + DEEP] = turned[0:half, :]
            sibs[h, :, n : n + DEEP] = turned[half:, :]
        beside(h).start()
    for h in range(2):
        at = h * mid
        beside(h).wait_recv()
        keep[:, at : at + mid] += sibr[h]
        for k in far:
            piece = keep[k * OWN : (k + 1) * OWN, at : at + mid]
            zsend[h * Z + k] = jnp.concatenate(
                [piece[:, :quarter], piece[:, quarter:]], axis=0).astype(BF16)
            along(h, k).start()
    for h in range(2):
        at = h * mid
        piece = keep[0:OWN, at : at + mid]
        result = jnp.concatenate([piece[:, :quarter], piece[:, quarter:]], axis=0)
        for k in range(1, Z):
            along(h, k).wait_recv()
            result = result + zrecv[h * Z + k].astype(F32)
        out[:, at : at + quarter] = result[0:OWN, :]
        out[:, at + quarter : at + mid] = result[OWN:, :]

    for d in range(4):
        @pl.when(has[d])
        def _(d=d):
            request(d).wait_send()
            for p in range(CMAX // 2):
                panels(d, p, d ^ 1).wait_send()
    for k in range(1, Q):
        owners(k).wait_send()
        spread(k).wait_send()
    for h in range(2):
        beside(h).wait_send()
        for k in range(1, Z):
            along(h, k).wait_send()


def shards(dims, basis, stiffness, inverse, coupling, panel_index, panel_count, owner_map):
    XH, Y, Z = dims
    Q = XH * Y * XL
    nco = OWN * XH * Y * CO * Z * XL
    m1 = CO * Z * OWN
    kp = KM + KR
    width = NB * PANEL
    n = CMAX // 2
    packed = -(-Q * KR // LW) * LW
    vmem = pl.BlockSpec(memory_space=pltpu.VMEM)
    smem = pl.BlockSpec(memory_space=pltpu.SMEM)
    hbm = pl.BlockSpec(memory_space=pl.ANY)
    dma = pltpu.SemaphoreType.DMA
    return pl.pallas_call(
        functools.partial(kernel, dims),
        out_shape=jax.ShapeDtypeStruct((OWN, nco), F32),
        in_specs=[vmem, smem, smem, vmem, hbm, hbm, hbm],
        out_specs=vmem,
        scratch_shapes=[
            pltpu.VMEM((kp, width), BF16),
            pltpu.VMEM((4, 8, LW), jnp.int32),
            pltpu.VMEM((2, 8, KM + LW), jnp.int32),
            pltpu.VMEM((4 * n, kp, 2 * PANEL), BF16),
            pltpu.VMEM((4 * n, kp, 2 * PANEL), BF16),
            pltpu.VMEM((4, 8, LW), jnp.int32),
            pltpu.VMEM((kp, width), F32),
            pltpu.VMEM((kp, width), F32),
            pltpu.VMEM((4, CMAX * PANEL, width), BF16),
            pltpu.VMEM((width, width), BF16),
            pltpu.VMEM((width, width), BF16),
            pltpu.VMEM((kp, width), BF16),
            pltpu.VMEM((kp, width), BF16),
            pltpu.VMEM((KM + LW, width), BF16),
            pltpu.VMEM((kp, KM + LW), BF16),
            pltpu.VMEM((nco, KM + LW), BF16),
            pltpu.VMEM((nco, Q * KM), BF16),
            pltpu.VMEM((nco, packed), BF16),
            pltpu.VMEM((Q, 8, KM + LW), jnp.int32),
            pltpu.VMEM((Q, kp, m1), BF16),
            pltpu.VMEM((Q, kp, m1), BF16),
            pltpu.VMEM((nco, m1), F32),
            pltpu.VMEM((m1 // 2, nco), F32),
            pltpu.VMEM((2, m1 // 2, nco // 2), F32),
            pltpu.VMEM((2, m1 // 2, nco // 2), F32),
            pltpu.VMEM((2 * Z, 2 * OWN, nco // 4), BF16),
            pltpu.VMEM((2 * Z, 2 * OWN, nco // 4), BF16),
            dma((6,)), dma((4,)), dma((4,)), dma((4 * n,)), dma((4 * n,)),
            dma((Q,)), dma((Q,)), dma((Q,)), dma((Q,)), dma((2,)), dma((2,)),
            dma((2 * Z,)), dma((2 * Z,)),
        ],
        compiler_params=pltpu.CompilerParams(
            collective_id=0, has_side_effects=True, vmem_limit_bytes=58 * 2**20
        ),
    )(basis[0, 0], panel_index[0, 0], panel_count[0], owner_map[0], inverse[0, 0], stiffness[0, 0], coupling[0, 0])


def solution(mesh):
    in_specs = (
        P("grp", "sub", None, None),
        P("grp", "sub", None, None),
        P("grp", "sub", None, None),
        P("grp", "sub", None, None, None),
        P("grp", "sub", None, None),
        P("grp", "sub", None),
        P("grp", "sub", None),
    )
    return jax.shard_map(
        functools.partial(shards, sizes(mesh.shape)),
        mesh=mesh, in_specs=in_specs, out_specs=P(("grp", "sub"), None), check_vma=False,
    )
```

```python
import functools

import jax
import jax.numpy as jnp
from jax import lax
from jax.experimental import pallas as pl
from jax.experimental.pallas import tpu as pltpu
from jax.sharding import PartitionSpec as P

K = 270
PANEL = 128
NB = 9
CMAX = 6
OWN = 8
KM = 256
KR = 16
LW = 128
WIDE = 384
DEEP = 256
XL = 2
CO = 2
MESH = pl.DeviceIdType.MESH
BF16 = jnp.bfloat16
F32 = jnp.float32


def sizes(mesh_shape):
    grp, sub = mesh_shape["grp"], mesh_shape["sub"]
    xh = 2 if grp >= 16 else 1
    return xh, grp // (xh * CO), sub // XL


def kernel(
    dims, basis, index, count, owner, inv_h, stiff_h, coup_h, out,
    basisp, reqs, own, psend, rows, rreq, acc, base, coup, inv, stiff, total, ext, proj, ct, rtp, rt, rtr,
    orecv, xsend, xrecv, acc2, keep, sibs, sibr, zsend, zrecv,
    lsem, rqs, rqr, ps, pr, os_, or_, xs, xr, ss, sr, zs, zr,
):
    XH, Y, Z = dims
    Q = XH * Y * XL
    G, S = XH * Y * CO, Z * XL
    nco = OWN * G * S
    m1 = CO * Z * OWN
    kp = KM + KR
    width = NB * PANEL
    g, s = lax.axis_index("grp"), lax.axis_index("sub")
    xh, y, co = g // (Y * CO), (g // CO) % Y, g % CO
    z, xl = s // XL, s % XL
    has = [g > 0, g < G - 1, s > 0, s < S - 1]
    face = [(g - 1, s), (g + 1, s), (g, s - 1), (g, s + 1)]
    plane = []
    for k in range(Q):
        a, b, c = k // (Y * XL), (k // XL) % Y, k % XL
        plane.append((((xh + a) % XH * Y + (y + b) % Y) * CO + co, z * XL + (xl + c) % XL))
    sibling = (g + 1 - 2 * co, s)
    column = [(g, (z + k) % Z * XL + xl) for k in range(Z)]

    loads = [pltpu.make_async_copy(coup_h.at[d], coup.at[d], lsem.at[d]) for d in range(4)]
    loads.append(pltpu.make_async_copy(inv_h, inv, lsem.at[4]))
    loads.append(pltpu.make_async_copy(stiff_h, stiff, lsem.at[5]))

    barrier = pltpu.get_barrier_semaphore()
    for d in range(4):
        @pl.when(has[d])
        def _(d=d):
            pl.semaphore_signal(barrier, inc=1, device_id=face[d], device_id_type=MESH)
    for peer in plane[1:] + [sibling] + column[1:]:
        pl.semaphore_signal(barrier, inc=1, device_id=peer, device_id_type=MESH)

    basisp[KM:kp, :] = jnp.zeros((KR, width), BF16)
    basisp[0:K, :] = basis[...]
    for d in range(4):
        @pl.when(jnp.logical_not(has[d]))
        def _(d=d):
            for p in range(CMAX // 2):
                rows[d * (CMAX // 2) + p] = jnp.zeros((kp, 2 * PANEL), BF16)
    for d in range(4):
        for c in range(CMAX):
            wanted = jnp.where(c < count[0, d], index[d, c], -1)
            reqs[d, c : c + 1, :] = jnp.full((1, LW), wanted, jnp.int32)
    own[0] = jnp.zeros((8, KM + LW), jnp.int32)
    own[0, 0:1, 0:K] = owner[...]
    m = jnp.broadcast_to(own[0, 0:1, :], (8, KM + LW))
    own[0] = m
    orecv[0] = m
    bits = [n.bit_length() - 1 for n in (XL, Z, CO, Y, XH)]
    ms, mg = m >> 3, m >> (3 + bits[0] + bits[1])
    there = ((mg >> (bits[2] + bits[3])) - xh) & (XH - 1)
    there = (there << bits[3]) + (((mg >> bits[2]) - y) & (Y - 1))
    there = (there << bits[0]) + ((ms - xl) & (XL - 1))
    there = (there << bits[2]) + ((mg - co) & (CO - 1))
    there = (there << bits[1]) + (((ms >> bits[0]) - z) & (Z - 1))
    own[1] = (there << 3) + (m & 7)

    faces = sum(h.astype(jnp.int32) for h in has)
    pl.semaphore_wait(barrier, faces + (Q - 1) + 1 + (Z - 1))

    def request(d):
        return pltpu.make_async_remote_copy(
            src_ref=reqs.at[d], dst_ref=rreq.at[d ^ 1], send_sem=rqs.at[d], recv_sem=rqr.at[d ^ 1],
            device_id=face[d], device_id_type=MESH)

    def request_in(d):
        return pltpu.make_async_remote_copy(
            src_ref=reqs.at[d], dst_ref=rreq.at[d], send_sem=rqs.at[d], recv_sem=rqr.at[d],
            device_id=face[d], device_id_type=MESH)

    def panels(d, p, into):
        n = CMAX // 2
        return pltpu.make_async_remote_copy(
            src_ref=psend.at[d * n + p], dst_ref=rows.at[into * n + p], send_sem=ps.at[d * n + p],
            recv_sem=pr.at[into * n + p], device_id=face[d], device_id_type=MESH)

    def owners(k):
        return pltpu.make_async_remote_copy(
            src_ref=own.at[0], dst_ref=orecv.at[k], send_sem=os_.at[k], recv_sem=or_.at[k],
            device_id=plane[k], device_id_type=MESH)

    def spread(k):
        return pltpu.make_async_remote_copy(
            src_ref=xsend.at[k], dst_ref=xrecv.at[k], send_sem=xs.at[k], recv_sem=xr.at[k],
            device_id=plane[k], device_id_type=MESH)

    def beside(h):
        return pltpu.make_async_remote_copy(
            src_ref=sibs.at[h], dst_ref=sibr.at[h], send_sem=ss.at[h], recv_sem=sr.at[h],
            device_id=sibling, device_id_type=MESH)

    def along(h, k):
        i = h * Z + k
        return pltpu.make_async_remote_copy(
            src_ref=zsend.at[i], dst_ref=zrecv.at[i], send_sem=zs.at[i], recv_sem=zr.at[i],
            device_id=column[k], device_id_type=MESH)

    order = (2, 3, 0, 1)
    for d in order:
        @pl.when(has[d])
        def _(d=d):
            request(d).start()
    for k in range(1, Q):
        owners(k).start()
    for load in loads:
        load.start()

    def own_rows(n, carry):
        at = pl.multiple_of(n * DEEP, DEEP)
        here = lax.broadcasted_iota(jnp.int32, (DEEP, KM + LW), 0) + at
        rtp[pl.ds(at, DEEP), :] = (own[1, 0:1, :] == here).astype(F32).astype(BF16)
        return carry

    acc[...] = jnp.zeros_like(acc)

    for p in range(CMAX // 2):
        for d in order:
            @pl.when(has[d])
            def _(d=d, p=p):
                if p == 0:
                    request_in(d).wait_recv()
                for h in range(2):
                    c = 2 * p + h
                    picked = None
                    for n in range(NB):
                        mark = (rreq[d, c : c + 1, 0:PANEL] == n).astype(F32).astype(BF16)
                        term = basisp[:, n * PANEL : (n + 1) * PANEL] * mark
                        picked = term if picked is None else picked + term
                    psend[d * (CMAX // 2) + p, :, h * PANEL : (h + 1) * PANEL] = picked
                panels(d, p, d ^ 1).start()

    lax.fori_loop(0, nco // DEEP, own_rows, 0)
    proj[...] = jnp.zeros_like(proj)

    for k in range(1, Q):
        owners(k).wait_recv()
    packed = []
    for first in range(0, Q, LW // KR):
        line = None
        for k in range(first, min(Q, first + LW // KR)):
            piece = orecv[k, :, KM : KM + LW]
            shift = (k - first) * KR
            piece = pltpu.roll(piece, shift, 1) if shift else piece
            line = piece if line is None else line + piece
        packed.append(line[0:1, :])

    def tables(n, carry):
        at = pl.multiple_of(n * DEEP, DEEP)
        here = lax.broadcasted_iota(jnp.int32, (DEEP, KM), 0) + at
        for k in range(Q):
            rt[pl.ds(at, DEEP), k * KM : (k + 1) * KM] = (
                (orecv[k, 0:1, 0:KM] == here).astype(F32).astype(BF16))
        narrow = lax.broadcasted_iota(jnp.int32, (DEEP, LW), 0) + at
        for i, line in enumerate(packed):
            rtr[pl.ds(at, DEEP), i * LW : (i + 1) * LW] = (line == narrow).astype(F32).astype(BF16)
        return carry

    lax.fori_loop(0, nco // DEEP, tables, 0)

    loads[4].wait()

    def inner(n, carry):
        at = pl.ds(pl.multiple_of(n * WIDE, WIDE), WIDE)
        base[:, at] = jnp.dot(basisp[...], inv[:, at], preferred_element_type=F32)
        return carry

    lax.fori_loop(0, width // WIDE, inner, 0)
    for d in range(4):
        loads[d].wait()
    for p in range(CMAX // 2):
        for d in (0, 1, 2, 3):
            i = d * (CMAX // 2) + p

            @pl.when(has[d])
            def _(d=d, p=p):
                panels(d, p, d).wait_recv()

            acc[...] += jnp.dot(
                rows[i], coup[d, 2 * PANEL * p : 2 * PANEL * (p + 1), :],
                preferred_element_type=F32)

    loads[5].wait()
    total[...] = acc[...].astype(BF16)

    outer = jnp.dot(total[...], inv[...], preferred_element_type=F32)
    ext[...] = (base[...] + outer).astype(BF16)
    proj[0:kp, :] = jnp.dot(ext[...], stiff[...], preferred_element_type=F32).astype(BF16)
    scale = float(width * K) ** (-0.5)
    ct[...] = (
        lax.dot_general(ext[...], proj[...], (((1,), (1,)), ((), ())), preferred_element_type=F32)
        * scale
    ).astype(BF16)

    for k in range(Q - 2, -1, -2):
        pair = lax.dot_general(
            ct[...], rtp[k * m1 : (k + 2) * m1, :], (((1,), (1,)), ((), ())),
            preferred_element_type=F32).astype(BF16)
        xsend[k + 1] = pair[:, m1:]
        spread(k + 1).start()
        xsend[k] = pair[:, :m1]
        if k:
            spread(k).start()
    xrecv[0] = xsend[0]

    def spread_from(k):
        return pltpu.make_async_remote_copy(
            src_ref=xsend.at[k], dst_ref=xrecv.at[k], send_sem=xs.at[k], recv_sem=xr.at[k],
            device_id=sibling, device_id_type=MESH)

    acc2[...] = jnp.dot(rt[:, 0:KM], xrecv[0, 0:KM, :], preferred_element_type=F32)

    def add(n, carry):
        k = Q - n
        spread_from(k).wait_recv()
        lanes = pl.ds(pl.multiple_of(k * KM, KM), KM)
        acc2[...] += jnp.dot(rt[:, lanes], xrecv[k, 0:KM, :], preferred_element_type=F32)
        return carry

    lax.fori_loop(1, Q, add, 0)
    rest = jnp.concatenate([xrecv[k, KM:kp, :] for k in range(Q)], axis=0)
    if rtr.shape[1] > Q * KR:
        rest = jnp.concatenate([rest, jnp.zeros((rtr.shape[1] - Q * KR, m1), BF16)], axis=0)

    half, mid, quarter = m1 // 2, nco // 2, nco // 4
    far = sorted(range(1, Z), key=lambda k: abs(2 * k - Z))
    for h in range(2):
        for n in range(0, mid, DEEP):
            at = h * mid + n
            last = jnp.dot(rtr[at : at + DEEP, :], rest, preferred_element_type=F32)
            turned = jnp.transpose(acc2[at : at + DEEP, :] + last)
            keep[:, at : at + DEEP] = turned[0:half, :]
            sibs[h, :, n : n + DEEP] = turned[half:, :]
        beside(h).start()
    for h in range(2):
        at = h * mid
        beside(h).wait_recv()
        keep[:, at : at + mid] += sibr[h]
        for k in far:
            piece = keep[k * OWN : (k + 1) * OWN, at : at + mid]
            zsend[h * Z + k] = jnp.concatenate(
                [piece[:, :quarter], piece[:, quarter:]], axis=0).astype(BF16)
            along(h, k).start()
    for h in range(2):
        at = h * mid
        piece = keep[0:OWN, at : at + mid]
        result = jnp.concatenate([piece[:, :quarter], piece[:, quarter:]], axis=0)
        for k in range(1, Z):
            along(h, k).wait_recv()
            result = result + zrecv[h * Z + k].astype(F32)
        out[:, at : at + quarter] = result[0:OWN, :]
        out[:, at + quarter : at + mid] = result[OWN:, :]

    for d in range(4):
        @pl.when(has[d])
        def _(d=d):
            request(d).wait_send()
            for p in range(CMAX // 2):
                panels(d, p, d ^ 1).wait_send()
    for k in range(1, Q):
        owners(k).wait_send()
        spread(k).wait_send()
    for h in range(2):
        beside(h).wait_send()
        for k in range(1, Z):
            along(h, k).wait_send()


def shards(dims, basis, stiffness, inverse, coupling, panel_index, panel_count, owner_map):
    XH, Y, Z = dims
    Q = XH * Y * XL
    nco = OWN * XH * Y * CO * Z * XL
    m1 = CO * Z * OWN
    kp = KM + KR
    width = NB * PANEL
    n = CMAX // 2
    packed = -(-Q * KR // LW) * LW
    vmem = pl.BlockSpec(memory_space=pltpu.VMEM)
    smem = pl.BlockSpec(memory_space=pltpu.SMEM)
    hbm = pl.BlockSpec(memory_space=pl.ANY)
    dma = pltpu.SemaphoreType.DMA
    return pl.pallas_call(
        functools.partial(kernel, dims),
        out_shape=jax.ShapeDtypeStruct((OWN, nco), F32),
        in_specs=[vmem, smem, smem, vmem, hbm, hbm, hbm],
        out_specs=vmem,
        scratch_shapes=[
            pltpu.VMEM((kp, width), BF16),
            pltpu.VMEM((4, 8, LW), jnp.int32),
            pltpu.VMEM((2, 8, KM + LW), jnp.int32),
            pltpu.VMEM((4 * n, kp, 2 * PANEL), BF16),
            pltpu.VMEM((4 * n, kp, 2 * PANEL), BF16),
            pltpu.VMEM((4, 8, LW), jnp.int32),
            pltpu.VMEM((kp, width), F32),
            pltpu.VMEM((kp, width), F32),
            pltpu.VMEM((4, CMAX * PANEL, width), BF16),
            pltpu.VMEM((width, width), BF16),
            pltpu.VMEM((width, width), BF16),
            pltpu.VMEM((kp, width), BF16),
            pltpu.VMEM((kp, width), BF16),
            pltpu.VMEM((KM + LW, width), BF16),
            pltpu.VMEM((kp, KM + LW), BF16),
            pltpu.VMEM((nco, KM + LW), BF16),
            pltpu.VMEM((nco, Q * KM), BF16),
            pltpu.VMEM((nco, packed), BF16),
            pltpu.VMEM((Q, 8, KM + LW), jnp.int32),
            pltpu.VMEM((Q, kp, m1), BF16),
            pltpu.VMEM((Q, kp, m1), BF16),
            pltpu.VMEM((nco, m1), F32),
            pltpu.VMEM((m1 // 2, nco), F32),
            pltpu.VMEM((2, m1 // 2, nco // 2), F32),
            pltpu.VMEM((2, m1 // 2, nco // 2), F32),
            pltpu.VMEM((2 * Z, 2 * OWN, nco // 4), BF16),
            pltpu.VMEM((2 * Z, 2 * OWN, nco // 4), BF16),
            dma((6,)), dma((4,)), dma((4,)), dma((4 * n,)), dma((4 * n,)),
            dma((Q,)), dma((Q,)), dma((Q,)), dma((Q,)), dma((2,)), dma((2,)),
            dma((2 * Z,)), dma((2 * Z,)),
        ],
        compiler_params=pltpu.CompilerParams(
            collective_id=0, has_side_effects=True, vmem_limit_bytes=58 * 2**20
        ),
    )(basis[0, 0], panel_index[0, 0], panel_count[0], owner_map[0], inverse[0, 0], stiffness[0, 0], coupling[0, 0])


def solution(mesh):
    in_specs = (
        P("grp", "sub", None, None),
        P("grp", "sub", None, None),
        P("grp", "sub", None, None),
        P("grp", "sub", None, None, None),
        P("grp", "sub", None, None),
        P("grp", "sub", None),
        P("grp", "sub", None),
    )
    return jax.shard_map(
        functools.partial(shards, sizes(mesh.shape)),
        mesh=mesh, in_specs=in_specs, out_specs=P(("grp", "sub"), None), check_vma=False,
    )
```
